256 devices in a mesh: dp: 16 (over z, core), mp: 4 (over y), pre: 4 (over x).
Axes of the slice: x: 4, y: 4, z: 8, core: 2. Of those that a mesh axis runs over, the one named last changes fastest.
Arguments:
- hidden: bfloat16 [16384, 6144], P(('dp', 'pre'), 'mp'), may hold values from -16 to 16
- grad_out: bfloat16 [16384, 8192], P(('dp', 'mp'), 'pre'), may hold values from -1 to 1
- block_owner: int32 [4, 4, 12, 1], P('mp', 'pre'), may hold values from 0 to 15; in each aligned block of 12 rows (0 to 11, 12 to 23, ..., all dimensions but the last counted through in order) at most 2 rows name the same one
- left_stat: bfloat16 [32, 2048, 2048], P('dp', 'mp', 'pre'), may hold values from -1 to 20, as said below
- right_stat: bfloat16 [32, 2048, 2048], P('dp', 'mp', 'pre'), may hold values from -1 to 20, as said below
- left_root: bfloat16 [32, 2048, 2048], P('dp', 'mp', 'pre'), may hold values from -1 to 2, as said below
- right_root: bfloat16 [32, 2048, 2048], P('dp', 'mp', 'pre'), may hold values from -1 to 2, as said below
Outputs:
- update: bfloat16 [6144, 8192], P('mp', 'pre')
The draws below stay inside these ranges and needn't reach their ends.
Inputs may be any that keep to these rules, and one draw needn't show every extreme that they name: `block_owner`: within the 12 blocks of one cell (one device's blocks), no owner is named more than 2 times, a bound that some block reaches. `left_stat`: each 512 x 512 tile is symmetric positive definite. `right_stat`: each 512 x 512 tile is symmetric positive definite. `left_root`: each 512 x 512 tile is symmetric. `right_root`: each 512 x 512 tile is symmetric.
All inputs are finite; a program needn't handle non-finite values.
Results may differ from the reference program's by a relative error of at most 0.025.
Values may be sent and summed in bfloat16 or wider, within the bound.
A program may use at most 128 MiB of HBM per device.

```python
import math
import jax
import jax.numpy as jnp
import numpy as np
from jax import lax

D = 8192
BLOCK = 512
BR = 3
TOK_LRN = 1024
BC = 4
FFW = 6144
TOKENS = 16384
CAP = 2
SLOTS = 32
N_DP = 16
N_MP = 4
N_PRE = 4


def tile_diagonal(key, low_value, high_value):
    key = jax.random.fold_in(key, 101)
    return jnp.exp(jax.random.uniform(key, (SLOTS, N_MP, BLOCK, N_PRE), jnp.float32, jnp.log(low_value), jnp.log(high_value)))


def tile_diagonal_right(key, low_value, high_value):
    key = jax.random.fold_in(key, 202)
    return jnp.exp(jax.random.uniform(key, (SLOTS, N_MP, BLOCK, N_PRE), jnp.float32, jnp.log(low_value), jnp.log(high_value)))


def symmetric_noise(key, spread):
    raw_noise = jax.random.uniform(key, (SLOTS, N_MP, BLOCK, N_PRE, BLOCK), jnp.float32, -spread, spread)
    return 0.5 * (raw_noise + jnp.swapaxes(raw_noise, 2, 4))


def tile_matrix(diag_values, noise):
    row_part = jnp.sqrt(diag_values)[:, :, :, :, None]
    col_part = jnp.sqrt(jnp.transpose(diag_values, (0, 1, 3, 2)))[:, :, None, :, :]
    row_ids = jnp.arange(BLOCK)[:, None, None]
    col_ids = jnp.arange(BLOCK)[None, None, :]
    unit = jnp.where(row_ids == col_ids, 1.0, 0.0).astype(jnp.float32)
    full = row_part * col_part * (unit[None, None] + noise)
    return full.reshape(SLOTS, N_MP * BLOCK, N_PRE * BLOCK)


def root_tiles(diag_values, key, low_jit, high_jit):
    key_jitter, key_noise = jax.random.split(key)
    jitter = jax.random.uniform(key_jitter, diag_values.shape, jnp.float32, low_jit, high_jit)
    root_diag = lax_quarter(0.8 * diag_values + 0.6) * jitter
    return tile_matrix(root_diag, symmetric_noise(key_noise, 0.03)).astype(jnp.bfloat16)


def lax_quarter(values):
    return jax.lax.rsqrt(jnp.sqrt(values))


def draw_hidden(key, part):
    key = jax.random.fold_in(key, 11)
    key_scale, key_value = jax.random.split(key)
    factor = jnp.exp(jax.random.uniform(key_scale, (FFW,), jnp.float32, 0.0, jnp.log(2.0)))
    values = jnp.clip(jax.random.normal(key_value, (TOKENS, FFW), jnp.float32), -6.0, 6.0)
    return (values * factor[None, :]).astype(jnp.bfloat16)


def draw_grad_out(key, part):
    key = jax.random.fold_in(key, 12)
    key_scale, key_value = jax.random.split(key)
    sigma = 0.68 / jnp.sqrt(jnp.float32(TOKENS * BLOCK))
    factor = jnp.exp(jax.random.uniform(key_scale, (D,), jnp.float32, 0.0, jnp.log(2.0)))
    values = jnp.clip(jax.random.normal(key_value, (TOKENS, D), jnp.float32), -6.0, 6.0)
    return (values * factor[None, :] * sigma).astype(jnp.bfloat16)


def draw_left_stat(key, part):
    diag_values = tile_diagonal(key, 1.0, 10.0)
    key = jax.random.fold_in(key, 21)
    return tile_matrix(diag_values, symmetric_noise(key, 0.03)).astype(jnp.bfloat16)


def draw_right_stat(key, part):
    diag_values = tile_diagonal_right(key, 1.0, 10.0)
    key = jax.random.fold_in(key, 23)
    return tile_matrix(diag_values, symmetric_noise(key, 0.03)).astype(jnp.bfloat16)


def draw_left_root(key, part):
    diag_values = tile_diagonal(key, 1.0, 10.0)
    key = jax.random.fold_in(key, 22)
    return root_tiles(diag_values, key, 0.9, 1.1)


def draw_right_root(key, part):
    diag_values = tile_diagonal_right(key, 1.0, 10.0)
    key = jax.random.fold_in(key, 24)
    return root_tiles(diag_values, key, 0.9, 1.1)


def deal_out(rng, own, number, rows, number_of, top, bound, skew):
    ranking = jax.random.permutation(rng, number_of)
    heavy_load, common = shares(number_of, rows * top, bound, skew, True), shares(number_of, rows * top, bound, skew, False)
    places = jnp.arange(number_of)

    def named(sizes, turn):
        used = int((sizes > 0).sum())
        fixed = max(1, used // 4)
        passed = fixed + (places - fixed + turn * (used - fixed)) % max(1, number_of - fixed)
        return jnp.zeros((number_of,), jnp.int32).at[ranking[jnp.where(places < fixed, places, passed)]].set(jnp.asarray(sizes, jnp.int32))

    sizes = jnp.where(number % 4 == 0, named(heavy_load, number // 4), named(common, number - number // 4 - 1))
    mixed = jax.random.permutation(jax.random.fold_in(own, 3), number_of)
    source_of, receiver = mixed[0:number_of // 2 * 2:2], mixed[1:number_of // 2 * 2:2]
    margin = jnp.minimum(sizes[source_of] - 1, bound - sizes[receiver]) // 2
    margin = jnp.where((source_of == ranking[0]) | (receiver == ranking[0]) | (sizes[receiver] == 0), 0, jnp.maximum(margin, 0))
    passed = jax.random.randint(jax.random.fold_in(own, 4), (number_of // 2,), 0, 1 << 20) % (margin + 1)
    sizes = sizes.at[source_of].add(-passed).at[receiver].add(passed)
    labels = jnp.searchsorted(jnp.cumsum(sizes), jnp.arange(rows * top), side="right").astype(jnp.int32)
    grid = labels.reshape(top, rows).T
    grid = grid[jax.random.permutation(jax.random.fold_in(own, 1), rows)]
    turn = jax.random.randint(jax.random.fold_in(own, 2), (rows, 1), 0, top)
    return jnp.take_along_axis(grid, (jnp.arange(top)[None, :] + turn) % top, axis=1)


def shares(count, total, limit, lean, full):
    loads = [(1 << 20) // math.isqrt(rank ** lean) + 1 for rank in range(1, count + 1)]
    largest = limit if full else min(limit, max(-(-total // count), total * loads[0] // sum(loads)))
    least = 1 if total - largest >= count - 1 else 0
    given, surplus = [largest] + [least] * (count - 1), total - largest - least * (count - 1)
    while surplus > 0:
        movable = [i for i in range(1, count) if given[i] < largest] or [i for i in range(1, count) if given[i] < limit]
        pool, remaining = sum([loads[i] for i in movable]), surplus
        for i in movable:
            addition = min(limit - given[i], max(1, remaining * loads[i] // pool), surplus)
            given[i] = given[i] + addition
            surplus = surplus - addition
    return np.array(given)


def setup_inputs(seed: int = 0) -> dict:
    key_of = jax.random.split(jax.random.key(seed), 8)
    hidden = draw_hidden(jax.random.fold_in(key_of[7], 71), 0)
    grad_out = draw_grad_out(jax.random.fold_in(key_of[7], 71), 0)
    block_owner_keys = jax.random.split(jax.random.fold_in(key_of[2], 1), N_MP * N_PRE * (BR * BC) // (BR * BC))
    block_owner_turns = jax.random.permutation(jax.random.fold_in(key_of[2], 3), N_MP * N_PRE * (BR * BC) // (BR * BC))
    block_owner = jax.vmap(lambda own, number: deal_out(jax.random.fold_in(key_of[2], 2), own, number, BR * BC, N_DP, 1, CAP, 2))(block_owner_keys, block_owner_turns).reshape((N_MP, N_PRE, BR * BC, 1))
    left_stat = draw_left_stat(jax.random.fold_in(key_of[7], 71), 0)
    right_stat = draw_right_stat(jax.random.fold_in(key_of[7], 71), 0)
    left_root = draw_left_root(jax.random.fold_in(key_of[7], 71), 0)
    right_root = draw_right_root(jax.random.fold_in(key_of[7], 71), 0)
    return dict(hidden=hidden, grad_out=grad_out, block_owner=block_owner, left_stat=left_stat, right_stat=right_stat, left_root=left_root, right_root=right_root)


def dot_high(left_arg, right_arg):
    return jnp.dot(left_arg, right_arg, precision=lax.Precision.HIGHEST, preferred_element_type=jnp.float32)

def inverse_root(root_tile, stat_tile):
    start = root_tile.astype(jnp.float32)
    square = dot_high(start, start)
    product = dot_high(square, stat_tile)
    fourth = dot_high(square, product)
    identity = jnp.eye(start.shape[0], dtype=jnp.float32)
    return dot_high(start, 5.0 * identity - fourth) * 0.25

def precondition(gradient, left_tile, right_tile, left_start, right_start):
    left_full = 0.8 * left_tile.astype(jnp.float32) + 0.2 * jnp.dot(gradient, gradient.T, preferred_element_type=jnp.float32)
    right_full = 0.8 * right_tile.astype(jnp.float32) + 0.2 * jnp.dot(gradient.T, gradient, preferred_element_type=jnp.float32)
    left_new = inverse_root(left_start, left_full)
    right_new = inverse_root(right_start, right_full)
    result = dot_high(dot_high(left_new, gradient.astype(jnp.float32)), right_new)
    inv_norm = lax.rsqrt(jnp.mean(result * result) + 1e-06)
    return (result * inv_norm).astype(jnp.bfloat16)

def reference(hidden, grad_out, block_owner, left_stat, right_stat, left_root, right_root):
    hid_learn = hidden.reshape(N_DP, TOK_LRN, FFW)
    out_learn = grad_out.reshape(N_DP, TOK_LRN, D)

    def add_learner(running, pair):
        hid_rows, out_rows = pair
        term = lax.dot_general(hid_rows, out_rows, (((0,), (0,)), ((), ())), preferred_element_type=jnp.float32)
        rounded = lax.optimization_barrier(term.astype(jnp.bfloat16))
        return (running + rounded.astype(jnp.float32), None)
    summed, _ = lax.scan(add_learner, jnp.zeros((FFW, D), jnp.float32), (hid_learn, out_learn))
    gradient = summed.astype(jnp.bfloat16)
    owners = block_owner.reshape(N_MP, N_PRE, BR * BC)
    per_cell = BR * BC

    def one_block(index):
        cell_m = index // (N_PRE * per_cell)
        cell_p = index // per_cell % N_PRE
        within = index % per_cell
        row_blk = within // BC
        col_blk = within % BC
        cell_owners = owners[cell_m, cell_p]
        owner_id = cell_owners[within]
        earlier = jnp.arange(per_cell, dtype=jnp.int32) < within
        position = jnp.sum(jnp.where(earlier & (cell_owners == owner_id), 1, 0)).astype(jnp.int32)
        slot_row = (owner_id * CAP + position).astype(jnp.int32)
        row_first = (cell_m * BLOCK).astype(jnp.int32)
        col_first = (cell_p * BLOCK).astype(jnp.int32)

        def tile_of(array):
            return lax.dynamic_slice(array, (slot_row, row_first, col_first), (1, BLOCK, BLOCK))[0]
        grad_block = lax.dynamic_slice(gradient, (((cell_m * BR + row_blk) * BLOCK).astype(jnp.int32), ((cell_p * BC + col_blk) * BLOCK).astype(jnp.int32)), (BLOCK, BLOCK))
        return precondition(grad_block, tile_of(left_stat), tile_of(right_stat), tile_of(left_root), tile_of(right_root))
    count = N_MP * N_PRE * per_cell
    results = lax.map(one_block, jnp.arange(count, dtype=jnp.int32))
    results = results.reshape(N_MP, N_PRE, BR, BC, BLOCK, BLOCK)
    return jnp.transpose(results, (0, 2, 4, 1, 3, 5)).reshape(FFW, D)
```

```python
import functools

import jax
import jax.numpy as jnp
from jax import lax
from jax.experimental import pallas as pl
from jax.experimental.pallas import tpu as pltpu
from jax.sharding import PartitionSpec as P

MESH = pl.DeviceIdType.MESH
F32 = jnp.float32
BF16 = jnp.bfloat16

BLOCK = 512
BR = 3
BC = 4
NB = BR * BC
CAP = 2
CHIPS = 8
TOK = 256

Q = 2
U = 2
ROWS = BLOCK // 4 // Q
M = NB * Q + 4 * U
LAGS = sorted({max(n * Q, U) for n in range(2 * CAP + 1)})

T_RS = 0
T_RSLAG = T_RS + 2 * M
T_FIN = T_RSLAG + 2
T_KSLOT = T_FIN + 2 * 4
T_AG = T_KSLOT + 4
T_AGLAG = T_AG + M
T_LEN = T_AGLAG + 1


def tables(owners, chip):
    k = jnp.arange(NB, dtype=jnp.int32)
    dest = owners // 2
    same_owner = (owners[:, None] == owners[None, :]) & (k[None, :] < k[:, None])
    slot = jnp.sum(same_owner.astype(jnp.int32), axis=1)
    same_chip = (dest[:, None] == dest[None, :]) & (k[None, :] < k[:, None])
    rank = jnp.sum(same_chip.astype(jnp.int32), axis=1)
    chips = jnp.arange(CHIPS, dtype=jnp.int32)
    count = jnp.sum((dest[None, :] == chips[:, None]).astype(jnp.int32), axis=1)
    places = jnp.maximum(count * Q, U)

    def before(start, target, sigma):
        gap = ((start - target) * sigma) % CHIPS
        gaps = ((start - chips) * sigma) % CHIPS
        return jnp.sum(jnp.where(gaps[None, :] < gap[:, None], places[None, :], 0), axis=1)

    piece = jnp.arange(Q, dtype=jnp.int32)
    j = jnp.arange(M, dtype=jnp.int32)
    code = (k[:, None] * Q + piece[None, :]).reshape(-1)
    rs, rslag, fin, pos = [], [], [], []
    local = owners % 2 * CAP + slot
    slots = jnp.arange(4, dtype=jnp.int32)
    here = (dest == chip)[None, :] & (local[None, :] == slots[:, None])
    own_places = jnp.sum(jnp.where(chips == chip, places, 0))
    for sigma in (1, -1):
        up = (chip - sigma) % CHIPS
        at = before((chip - sigma) % CHIPS, dest, sigma) + rank * Q
        at = (at[:, None] + piece[None, :]).reshape(-1)
        rs.append(jnp.sum(jnp.where(at[None, :] == j[:, None], code[None, :], 0), axis=1))
        rslag.append(jnp.sum(jnp.where(chips == up, places, 0))[None])
        last = before((up - sigma) % CHIPS, dest, sigma) + rank * Q
        fin.append(jnp.sum(jnp.where(here, last[None, :], 0), axis=1))
        arrive = before(up, dest, sigma) + rank * Q
        pos.append(jnp.where(dest == chip, M + local * Q, arrive))
    kslot = jnp.sum(jnp.where(here, k[None, :], 0), axis=1)
    own_at = (rank[:, None] * Q + piece[None, :]).reshape(-1)
    own_code = (local[:, None] * Q + piece[None, :]).reshape(-1)
    own_here = jnp.repeat(dest == chip, Q)
    ag = jnp.sum(
        jnp.where((own_at[None, :] == j[:, None]) & own_here[None, :], own_code[None, :], 0), axis=1
    )
    table = jnp.concatenate(rs + rslag + fin + [kslot, ag, own_places[None]])
    return table.astype(jnp.int32), jnp.concatenate(pos).astype(jnp.int32)


def split(value):
    high = value.astype(BF16)
    return high, (value - high.astype(F32)).astype(BF16)


def mm(a, b):
    return jnp.dot(a, b, preferred_element_type=F32)


def mm_t(a, b):
    return lax.dot_general(a, b, (((0,), (0,)), ((), ())), preferred_element_type=F32)


def fifth(x, stat):
    sh, sl = split(mm(x, x))
    qh, ql = split(mm(sh, sh) + mm(sh, sl) + mm(sl, sh))
    x5 = mm(qh, x) + mm(ql, x)
    h, low = split(x5)
    return 1.25 * x.astype(F32) - 0.2 * (mm(h, stat) + mm(low, stat)), 0.05 * x5


def main_kernel(
    tab, hid, gro, ls, rs, lr, rr, out,
    hb, gb, pb, eb, sb, ssend, srecv, arecv, gfull, gx, own4, res, stats, ops, cf,
    local_sem, x_send, x_recv, y_send, y_recv, pe_send, pe_recv,
    s_send, s_recv, a_send, a_recv, gx_send, gx_recv, o_send, o_recv,
    f_local, f_send, f_recv, t_local, t_send, t_recv,
):
    dp = lax.axis_index("dp")
    mp = lax.axis_index("mp")
    pre = lax.axis_index("pre")
    chip = dp // 2
    core = lax.rem(dp, 2)
    mate = 1 - core
    peer = {"dp": chip * 2 + mate}
    x_to = [{"pre": lax.rem(pre + 1, 4)}, {"pre": lax.rem(pre + 3, 4)}]
    y_to = [{"mp": lax.rem(mp + 1, 4)}, {"mp": lax.rem(mp + 3, 4)}]
    z_to = [
        {"dp": lax.rem(chip + 1, CHIPS) * 2 + core},
        {"dp": lax.rem(chip + CHIPS - 1, CHIPS) * 2 + core},
    ]

    def remote(src, dst, send, recv, to):
        return pltpu.make_async_remote_copy(
            src_ref=src, dst_ref=dst, send_sem=send, recv_sem=recv, device_id=to, device_id_type=MESH
        )

    locals_ = []
    for i, src in enumerate((ls, rs, lr, rr)):
        locals_.append(pltpu.make_async_copy(src, stats.at[i], local_sem.at[i]))
    for r in range(BR):
        locals_.append(
            pltpu.make_async_copy(
                hid.at[:, pl.ds(r * BLOCK, BLOCK)], hb.at[r, pl.ds(pre * TOK, TOK)], local_sem.at[4 + r]
            )
        )
    for c in range(BC):
        locals_.append(
            pltpu.make_async_copy(
                gro.at[:, pl.ds(c * BLOCK, BLOCK)], gb.at[c, pl.ds(mp * TOK, TOK)], local_sem.at[7 + c]
            )
        )
    for copy in locals_:
        copy.start()

    barrier = pltpu.get_barrier_semaphore()
    for to in [peer] + x_to + y_to + z_to:
        pl.semaphore_signal(barrier, inc=1, device_id=to, device_id_type=MESH)
    pl.semaphore_wait(barrier, 7)

    def gather(src, buf, me, to, send, recv):
        def direct(i, way):
            return remote(
                src.at[:, pl.ds(i * BLOCK, BLOCK)],
                buf.at[i, pl.ds(me * TOK, TOK)],
                send.at[i, way], recv.at[i, way], to[way],
            )

        def arrived(i, way):
            who = lax.rem(me + (3 if way == 0 else 1), 4)
            part = buf.at[i, pl.ds(who * TOK, TOK)]
            return remote(part, part, send.at[i, way], recv.at[i, way], to[way])

        def forward(i, way):
            who = lax.rem(me + (3 if way == 0 else 1), 4)
            part = buf.at[i, pl.ds(who * TOK + way * (TOK // 2), TOK // 2)]
            return remote(part, part, send.at[i, 2 + way], recv.at[i, 2 + way], to[way])

        def far(i, way):
            who = lax.rem(me + 2, 4)
            part = buf.at[i, pl.ds(who * TOK + way * (TOK // 2), TOK // 2)]
            return remote(part, part, send.at[i, 2 + way], recv.at[i, 2 + way], to[way])

        return direct, arrived, forward, far

    rings = [
        (BR, gather(hid, hb, pre, x_to, x_send, x_recv)),
        (BC, gather(gro, gb, mp, y_to, y_send, y_recv)),
    ]

    def start_direct(i):
        for count, (direct, _, _, _) in rings:
            if i < count:
                for way in range(2):
                    direct(i, way).start()

    def pass_on(i):
        for count, (_, arrived, forward, _) in rings:
            if i < count:
                for way in range(2):
                    arrived(i, way).wait_recv()
                    forward(i, way).start()

    def finish(i):
        for count, (_, _, _, far) in rings:
            if i < count:
                for way in range(2):
                    far(i, way).wait_recv()

    def operators(side, s):
        a, b = fifth(stats[2 + side, s], stats[side, s])
        if side == 0:
            ops[s, 0], ops[s, 1] = split(a)
            ops[s, 2], ops[s, 3] = split(b)
        else:
            cf[s] = a
            ops[s, 4], ops[s, 5] = split(b)

    def to_mate(k):
        return remote(pb.at[k, mate], eb.at[k], pe_send.at[k], pe_recv.at[k], peer)

    def partial(r, c):
        k = r * BC + c
        value = mm_t(hb[r], gb[c]).astype(BF16)
        pb[k] = value.reshape(2, 2 * Q, ROWS, BLOCK)
        to_mate(k).start()

    def chunk_products(i):
        if i < BR:
            lax.fori_loop(0, i + 1, lambda c, _: (partial(i, c), 0)[1], 0)
        if i > 0:
            lax.fori_loop(0, min(i, BR), lambda r, _: (partial(r, i), 0)[1], 0)

    start_direct(0)
    start_direct(1)
    for copy in locals_[:4]:
        copy.wait()
    units = [(0, 0), (1, 0), (0, 1), (1, 1)]
    operators(*units[0])
    for copy in locals_[4:]:
        copy.wait()
    for i in range(BC):
        pass_on(i)
        if i + 2 < BC:
            start_direct(i + 2)
        if i + 1 < len(units):
            operators(*units[i + 1])
        finish(i)
        chunk_products(i)

    def add_halves(k, _):
        to_mate(k).wait_recv()
        for way in range(2):
            total = pb[k, core, pl.ds(way * Q, Q)].astype(F32) + eb[k, pl.ds(way * Q, Q)].astype(F32)
            sb[way, pl.ds(k * Q, Q)] = total.astype(BF16)
        return 0

    lax.fori_loop(0, NB, add_halves, 0)

    def s_copy(way, j):
        return remote(ssend.at[way, j], srecv.at[way, j], s_send.at[way, j], s_recv.at[way, j], z_to[way])

    def a_copy(way, j):
        return remote(ssend.at[way, j], arecv.at[way, j], a_send.at[way, j], a_recv.at[way, j], z_to[way])

    def delayed(buf, way, j, lag):
        value = buf[way, lax.max(j - LAGS[0], 0)]
        for candidate in LAGS[1:]:
            value = jnp.where(lag == candidate, buf[way, lax.max(j - candidate, 0)], value)
        return value

    def reduce_step(j, first):
        for way in range(2):
            own = sb[way, tab[T_RS + way * M + j]]
            if first:
                ssend[way, j] = own
            else:
                s_copy(way, j - U).wait_recv()
                lag = tab[T_RSLAG + way]
                came = delayed(srecv, way, j, lag).astype(F32)
                total = own.astype(F32) + jnp.where(j >= lag, came, 0.0)
                ssend[way, j] = total.astype(BF16)
            s_copy(way, j).start()

    for j in range(U):
        reduce_step(j, True)
    lax.fori_loop(U, M, lambda j, _: (reduce_step(j, False), 0)[1], 0)
    for way in range(2):
        for j in range(M - U, M):
            s_copy(way, j).wait_recv()

    def final(way, place, i):
        came = srecv[way, tab[T_FIN + way * 4 + place] + i].astype(F32)
        own = sb[way, tab[T_KSLOT + place] * Q + i].astype(F32)
        return (came + own).astype(BF16)

    def gx_copy(s):
        return remote(gx.at[s], gfull.at[s, core], gx_send.at[s], gx_recv.at[s], peer)

    for s in range(CAP):
        for way in range(2):
            for i in range(Q):
                gx[s, way * Q + i] = final(way, mate * CAP + s, i)
        gx_copy(s).start()
    for s in range(CAP):
        for way in range(2):
            for i in range(Q):
                gfull[s, core, way * Q + i] = final(way, core * CAP + s, i)

    def drain(j, _):
        for way in range(2):
            s_copy(way, j).wait_send()
        return 0

    def o_copy(s):
        place = core * CAP + s
        return remote(res.at[s, mate], own4.at[place], o_send.at[s], o_recv.at[s], peer)

    def o_arrive(s):
        place = mate * CAP + s
        return remote(res.at[s, mate], own4.at[place], o_send.at[s], o_recv.at[s], peer)

    for s in range(CAP):
        remote(gx.at[s], gfull.at[s, mate], gx_send.at[s], gx_recv.at[s], peer).wait_recv()
        g = gfull[s].reshape(BLOCK, BLOCK)
        gh, gl = split(mm_t(g, g))
        ggh, ggl = split(mm(g, gh) + mm(g, gl))
        m = mm(ops[s, 0], g) + mm(ops[s, 1], g)
        m = m - (mm(ops[s, 2], ggh) + mm(ops[s, 2], ggl) + mm(ops[s, 3], ggh))
        n = cf[s] - (mm(ops[s, 4], gh) + mm(ops[s, 4], gl) + mm(ops[s, 5], gh))
        mh, ml = split(m)
        nh, nl = split(n)
        p = mm(mh, nh) + mm(mh, nl) + mm(ml, nh)
        inv = lax.rsqrt(jnp.sum(p * p, keepdims=True) * (1.0 / (BLOCK * BLOCK)) + 1e-06)
        res[s] = (p * inv).astype(BF16).reshape(2, 2 * Q, ROWS, BLOCK)
        o_copy(s).start()
        own4[core * CAP + s] = res[s, core]

    lax.fori_loop(0, M, drain, 0)

    def f_here(way, j):
        return pltpu.make_async_copy(arecv.at[way, j], out.at[way, j, core], f_local.at[way, j])

    def f_mate(way, j, half):
        return remote(arecv.at[way, j], out.at[way, j, half], f_send.at[way, j], f_recv.at[way, j], peer)

    def t_here(way, place):
        return pltpu.make_async_copy(
            own4.at[place, pl.ds(way * Q, Q)], out.at[way, pl.ds(M + place * Q, Q), core], t_local.at[way, place]
        )

    def t_mate(way, place, half):
        return remote(
            own4.at[place, pl.ds(way * Q, Q)], out.at[way, pl.ds(M + place * Q, Q), half],
            t_send.at[way, place], t_recv.at[way, place], peer,
        )

    for s in range(CAP):
        o_arrive(s).wait_recv()

    def own_piece(way, j):
        code = tab[T_AG + j]
        return own4[code // Q, way * Q + lax.rem(code, Q)]

    def spread(way, j):
        f_here(way, j).start()
        f_mate(way, j, core).start()

    def gather_step(j, first):
        for way in range(2):
            own = own_piece(way, j)
            if first:
                ssend[way, j] = own
            else:
                a_copy(way, j - U).wait_recv()
                lag = tab[T_AGLAG]
                ssend[way, j] = jnp.where(j >= lag, delayed(arecv, way, j, lag), own)
            a_copy(way, j).start()
            if not first:
                spread(way, j - U)

    for j in range(U):
        gather_step(j, True)
    for way in range(2):
        for place in range(2 * CAP):
            t_here(way, place).start()
            t_mate(way, place, core).start()
    lax.fori_loop(U, M, lambda j, _: (gather_step(j, False), 0)[1], 0)
    for way in range(2):
        for j in range(M - U, M):
            a_copy(way, j).wait_recv()
            spread(way, j)

    def drain_all(j, _):
        for way in range(2):
            a_copy(way, j).wait_send()
            f_here(way, j).wait()
            f_mate(way, j, core).wait_send()
            f_mate(way, j, mate).wait_recv()
        return 0

    lax.fori_loop(0, M, drain_all, 0)
    for way in range(2):
        for place in range(2 * CAP):
            t_here(way, place).wait()
            t_mate(way, place, core).wait_send()
            t_mate(way, place, mate).wait_recv()
    for count, (direct, _, forward, _) in rings:
        for i in range(count):
            for way in range(2):
                direct(i, way).wait_send()
                forward(i, way).wait_send()
    lax.fori_loop(0, NB, lambda k, _: (to_mate(k).wait_send(), 0)[1], 0)
    for s in range(CAP):
        gx_copy(s).wait_send()
        o_copy(s).wait_send()


def run_main(table, hidden, grad_out, left_stat, right_stat, left_root, right_root):
    dma = pltpu.SemaphoreType.DMA
    anywhere = pl.BlockSpec(memory_space=pl.ANY)
    stream = pltpu.VMEM((2, M, ROWS, BLOCK), BF16)
    return pl.pallas_call(
        main_kernel,
        out_shape=jax.ShapeDtypeStruct((2, M + 4 * Q, 2, ROWS, BLOCK), BF16),
        in_specs=[pl.BlockSpec(memory_space=pltpu.SMEM)] + [anywhere] * 6,
        out_specs=anywhere,
        scratch_shapes=[
            pltpu.VMEM((BR, 4 * TOK, BLOCK), BF16),
            pltpu.VMEM((BC, 4 * TOK, BLOCK), BF16),
            pltpu.VMEM((NB, 2, 2 * Q, ROWS, BLOCK), BF16),
            pltpu.VMEM((NB, 2 * Q, ROWS, BLOCK), BF16),
            pltpu.VMEM((2, NB * Q, ROWS, BLOCK), BF16),
            stream,
            stream,
            stream,
            pltpu.VMEM((CAP, 2, 2 * Q, ROWS, BLOCK), BF16),
            pltpu.VMEM((CAP, 2 * Q, ROWS, BLOCK), BF16),
            pltpu.VMEM((2 * CAP, 2 * Q, ROWS, BLOCK), BF16),
            pltpu.VMEM((CAP, 2, 2 * Q, ROWS, BLOCK), BF16),
            pltpu.VMEM((4, CAP, BLOCK, BLOCK), BF16),
            pltpu.VMEM((CAP, 6, BLOCK, BLOCK), BF16),
            pltpu.VMEM((CAP, BLOCK, BLOCK), F32),
            dma((11,)),
            dma((BR, 4)), dma((BR, 4)), dma((BC, 4)), dma((BC, 4)),
            dma((NB,)), dma((NB,)),
            dma((2, M)), dma((2, M)), dma((2, M)), dma((2, M)),
            dma((CAP,)), dma((CAP,)), dma((CAP,)), dma((CAP,)),
            dma((2, M)), dma((2, M)), dma((2, M)),
            dma((2, 2 * CAP)), dma((2, 2 * CAP)), dma((2, 2 * CAP)),
        ],
        compiler_params=pltpu.CompilerParams(
            collective_id=0, has_side_effects=True, vmem_limit_bytes=60 * 1024 * 1024
        ),
        name="main",
    )(table, hidden, grad_out, left_stat, right_stat, left_root, right_root)


def lay_out_kernel(pos, pieces, out, buf, in_sem, out_sem):
    def read(k, way):
        return pltpu.make_async_copy(
            pieces.at[way, pl.ds(pos[way * NB + k], Q)], buf.at[k, way], in_sem.at[k, way]
        )

    def write(k, half, way, i):
        r, c = k // BC, k % BC
        row = r * BLOCK + half * (BLOCK // 2) + way * (BLOCK // 4) + i * ROWS
        return pltpu.make_async_copy(
            buf.at[k, way, i, half],
            out.at[pl.ds(row, ROWS), pl.ds(c * BLOCK, BLOCK)],
            out_sem.at[k, half, way, i],
        )

    parts = [(half, way, i) for half in range(2) for way in range(2) for i in range(Q)]
    for k in range(NB):
        for way in range(2):
            read(k, way).start()
    for k in range(NB):
        for way in range(2):
            read(k, way).wait()
        for half, way, i in parts:
            write(k, half, way, i).start()
    for k in range(NB):
        for half, way, i in parts:
            write(k, half, way, i).wait()


def run_lay_out(pos, pieces):
    dma = pltpu.SemaphoreType.DMA
    return pl.pallas_call(
        lay_out_kernel,
        out_shape=jax.ShapeDtypeStruct((BR * BLOCK, BC * BLOCK), BF16),
        in_specs=[pl.BlockSpec(memory_space=pltpu.SMEM), pl.BlockSpec(memory_space=pl.ANY)],
        out_specs=pl.BlockSpec(memory_space=pl.ANY),
        scratch_shapes=[
            pltpu.VMEM((NB, 2, Q, 2, ROWS, BLOCK), BF16),
            dma((NB, 2)),
            dma((NB, 2, 2, Q)),
        ],
        compiler_params=pltpu.CompilerParams(vmem_limit_bytes=32 * 1024 * 1024),
        name="lay_out",
    )(pos, pieces)


def shards(hidden, grad_out, block_owner, left_stat, right_stat, left_root, right_root):
    table, pos = tables(block_owner.reshape(NB), lax.axis_index("dp") // 2)
    pieces = run_main(table, hidden, grad_out, left_stat, right_stat, left_root, right_root)
    return run_lay_out(pos, pieces)


def solution(mesh):
    in_specs = (
        P(("dp", "pre"), "mp"),
        P(("dp", "mp"), "pre"),
        P("mp", "pre", None, None),
        P("dp", "mp", "pre"),
        P("dp", "mp", "pre"),
        P("dp", "mp", "pre"),
        P("dp", "mp", "pre"),
    )
    return jax.shard_map(
        shards, mesh=mesh, in_specs=in_specs, out_specs=P("mp", "pre"), check_vma=False
    )
```

```python
import jax
import jax.numpy as jnp
from jax import lax
from jax.experimental import pallas as pl
from jax.experimental.pallas import tpu as pltpu
from jax.sharding import PartitionSpec as P

MESH = pl.DeviceIdType.MESH
F32 = jnp.float32
BF16 = jnp.bfloat16

BLOCK = 512
BR = 3
BC = 4
NB = BR * BC
CAP = 2
CHIPS = 8
TOK = 256

Q = 2
U = 3
ROWS = BLOCK // 4 // Q
Z = max(2 * CAP * Q, U)
M = NB * Q + 4 * U
B = 4
assert M % B == 0 and Q * 2 >= U


def split(value):
    high = value.astype(BF16)
    return high, (value - high.astype(F32)).astype(BF16)


def mm(a, b):
    return jnp.dot(a, b, preferred_element_type=F32)


def mm_t(a, b):
    return lax.dot_general(a, b, (((0,), (0,)), ((), ())), preferred_element_type=F32)


def fifth(x, stat):
    sh, sl = split(mm(x, x))
    qh, ql = split(mm(sh, sh) + mm(sh, sl) + mm(sl, sh))
    x5 = mm(qh, x) + mm(ql, x)
    h, low = split(x5)
    return 1.25 * x.astype(F32) - 0.2 * (mm(h, stat) + mm(low, stat)), 0.05 * x5


def total(terms):
    result = terms[0]
    for term in terms[1:]:
        result = result + term
    return result


def make_tables(owner_ref, chip, places_ref, before_ref, rs_ref, fin_ref, kslot_ref, ag_ref, lag_ref, pos_ref):
    i32 = jnp.int32
    owner = [owner_ref[k] for k in range(NB)]
    dest = [lax.div(o, 2) for o in owner]

    def ones(flags):
        return total([f.astype(i32) for f in flags]) if flags else jnp.int32(0)

    slot = [jnp.minimum(ones([owner[e] == owner[k] for e in range(k)]), CAP - 1) for k in range(NB)]
    rank = [jnp.minimum(ones([dest[e] == dest[k] for e in range(k)]), 2 * CAP - 1) for k in range(NB)]
    local = [lax.rem(owner[k], 2) * CAP + slot[k] for k in range(NB)]
    for d in range(CHIPS):
        places_ref[d] = jnp.clip(ones([dest[k] == d for k in range(NB)]) * Q, U, Z)
    mine = places_ref[chip]
    lag_ref[2] = mine
    here = [(dest[k] == chip).astype(i32) for k in range(NB)]
    for s in range(2 * CAP):
        kslot_ref[s] = jnp.minimum(
            total([here[k] * (local[k] == s).astype(i32) * k for k in range(NB)]), NB - 1
        )
    for way, sigma in enumerate((1, -1)):
        near = [places_ref[lax.rem(chip + CHIPS - g * sigma, CHIPS)] for g in range(CHIPS)]
        lag_ref[way] = near[1]
        running = jnp.int32(0)
        for g in range(1, CHIPS):
            before_ref[g] = running
            running = running + near[g]
        before_ref[0] = running
        spot = []
        for k in range(NB):
            gap = lax.rem((chip - dest[k]) * sigma + CHIPS, CHIPS)
            spot.append(before_ref[gap] + rank[k] * Q)
            pos_ref[way * NB + k] = jnp.where(here[k] == 1, M + local[k] * Q, jnp.minimum(spot[k], M - Q))
        for s in range(2 * CAP):
            last = total(
                [here[k] * (local[k] == s).astype(i32) * (running - near[1] + rank[k] * Q) for k in range(NB)]
            )
            fin_ref[way * 2 * CAP + s] = jnp.minimum(last, M - Q)

        def piece_of(j, _):
            codes = []
            for k in range(NB):
                off = j - spot[k]
                codes.append(jnp.where((off >= 0) & (off < Q), k * Q + off, 0))
            rs_ref[way * M + j] = jnp.minimum(total(codes), NB * Q - 1)
            return 0

        lax.fori_loop(0, M, piece_of, 0)
    for i in range(Z):
        codes = []
        for k in range(NB):
            off = i - Z + mine - rank[k] * Q
            codes.append(jnp.where((here[k] == 1) & (off >= 0) & (off < Q), local[k] * Q + off, 0))
        ag_ref[i] = jnp.minimum(total(codes), 2 * CAP * Q - 1)


def main_kernel(
    owner_ref, hid, gro, ls, rs, lr, rr, out, pos_ref,
    hb, gb, pb, eb, sb, ssend, srecv, arecv, shadow, gfull, gx, own4, res, stats, ops, cf,
    places_ref, before_ref, rs_ref, fin_ref, kslot_ref, ag_ref, lag_ref,
    local_sem, x_send, x_recv, y_send, y_recv, pe_send, pe_recv,
    s_send, s_recv, a_send, a_recv, gx_send, gx_recv, o_send, o_recv,
    f_local, f_send, f_recv, t_local, t_send, t_recv,
):
    dp = lax.axis_index("dp")
    mp = lax.axis_index("mp")
    pre = lax.axis_index("pre")
    chip = dp // 2
    core = lax.rem(dp, 2)
    mate = 1 - core
    peer = {"dp": chip * 2 + mate}
    x_to = [{"pre": lax.rem(pre + 1, 4)}, {"pre": lax.rem(pre + 3, 4)}]
    y_to = [{"mp": lax.rem(mp + 1, 4)}, {"mp": lax.rem(mp + 3, 4)}]
    z_to = [
        {"dp": lax.rem(chip + 1, CHIPS) * 2 + core},
        {"dp": lax.rem(chip + CHIPS - 1, CHIPS) * 2 + core},
    ]

    def remote(src, dst, send, recv, to):
        return pltpu.make_async_remote_copy(
            src_ref=src, dst_ref=dst, send_sem=send, recv_sem=recv, device_id=to, device_id_type=MESH
        )

    stat_copies = [
        pltpu.make_async_copy(src, stats.at[i], local_sem.at[i]) for i, src in enumerate((ls, rs, lr, rr))
    ]
    token_copies = []
    for i in range(BC):
        if i < BR:
            token_copies.append(
                pltpu.make_async_copy(
                    hid.at[:, pl.ds(i * BLOCK, BLOCK)], hb.at[i, pl.ds(pre * TOK, TOK)], local_sem.at[4 + i]
                )
            )
        token_copies.append(
            pltpu.make_async_copy(
                gro.at[:, pl.ds(i * BLOCK, BLOCK)], gb.at[i, pl.ds(mp * TOK, TOK)], local_sem.at[7 + i]
            )
        )
    for copy in token_copies + stat_copies:
        copy.start()

    barrier = pltpu.get_barrier_semaphore()
    for to in [peer] + x_to + y_to + z_to:
        pl.semaphore_signal(barrier, inc=1, device_id=to, device_id_type=MESH)
    pl.semaphore_wait(barrier, 7)

    def gather(src, buf, me, to, send, recv):
        def direct(i, way):
            return remote(
                src.at[:, pl.ds(i * BLOCK, BLOCK)],
                buf.at[i, pl.ds(me * TOK, TOK)],
                send.at[0], recv.at[i, way], to[way],
            )

        def arrived(i, way):
            who = lax.rem(me + (3 if way == 0 else 1), 4)
            part = buf.at[i, pl.ds(who * TOK, TOK)]
            return remote(part, part, send.at[0], recv.at[i, way], to[way])

        def forward(i, way):
            who = lax.rem(me + (3 if way == 0 else 1), 4)
            part = buf.at[i, pl.ds(who * TOK + way * (TOK // 2), TOK // 2)]
            return remote(part, part, send.at[0], recv.at[i, 2 + way], to[way])

        def far(i, way):
            who = lax.rem(me + 2, 4)
            part = buf.at[i, pl.ds(who * TOK + way * (TOK // 2), TOK // 2)]
            return remote(part, part, send.at[0], recv.at[i, 2 + way], to[way])

        return direct, arrived, forward, far

    rings = [
        (BR, gather(hid, hb, pre, x_to, x_send, x_recv)),
        (BC, gather(gro, gb, mp, y_to, y_send, y_recv)),
    ]

    def start_direct(i):
        for count, (direct, _, _, _) in rings:
            if i < count:
                for way in range(2):
                    direct(i, way).start()

    def pass_on(i):
        for count, (_, arrived, forward, _) in rings:
            if i < count:
                for way in range(2):
                    arrived(i, way).wait_recv()
                    forward(i, way).start()

    def finish(i):
        for count, (_, _, _, far) in rings:
            if i < count:
                for way in range(2):
                    far(i, way).wait_recv()

    def operators(side, s):
        a, b = fifth(stats[2 + side, s], stats[side, s])
        if side == 0:
            ops[s, 0], ops[s, 1] = split(a)
            ops[s, 2] = b.astype(BF16)
        else:
            cf[s] = a
            ops[s, 3] = b.astype(BF16)

    def to_mate(k):
        return remote(pb.at[k, mate], eb.at[k], pe_send.at[0], pe_recv.at[k], peer)

    def partial(r, c):
        k = r * BC + c
        value = mm_t(hb[r], gb[c]).astype(BF16)
        pb[k] = value.reshape(2, 2 * Q, ROWS, BLOCK)
        to_mate(k).start()

    def add_halves(r, c):
        k = r * BC + c
        to_mate(k).wait_recv()
        for way in range(2):
            both = pb[k, core, pl.ds(way * Q, Q)].astype(F32) + eb[k, pl.ds(way * Q, Q)].astype(F32)
            sb[way, pl.ds(k * Q, Q)] = both.astype(BF16)

    def for_chunk(i, what):
        if i < BR:
            lax.fori_loop(0, i + 1, lambda c, _: (what(i, c), 0)[1], 0)
        if i > 0:
            lax.fori_loop(0, min(i, BR), lambda r, _: (what(r, i), 0)[1], 0)

    def between(i):
        if i == 0:
            for copy in stat_copies:
                copy.wait()
            operators(0, 0)
        elif i == 1:
            operators(1, 0)
            for way in range(2):
                shadow[way, pl.ds(0, Z)] = jnp.zeros((Z, ROWS, BLOCK), BF16)
        elif i == 2:
            make_tables(
                owner_ref, chip, places_ref, before_ref, rs_ref, fin_ref, kslot_ref, ag_ref, lag_ref, pos_ref
            )
            operators(0, 1)
        elif i == 3:
            operators(1, 1)

    start_direct(0)
    start_direct(1)
    for copy in token_copies:
        copy.wait()
    between(0)
    for i in range(BC + 1):
        if i < BC:
            pass_on(i)
            if i + 2 < BC:
                start_direct(i + 2)
            if i + 1 < BC:
                between(i + 1)
        if i > 0:
            finish(i - 1)
            for_chunk(i - 1, partial)
        if i > 1:
            for_chunk(i - 2, add_halves)
    for_chunk(BC - 1, add_halves)

    def s_copy(way, j):
        return remote(ssend.at[way, j], srecv.at[way, j], s_send.at[way], s_recv.at[way, j], z_to[way])

    def a_copy(way, j):
        return remote(ssend.at[way, j], arecv.at[way, j], a_send.at[way], a_recv.at[way, j], z_to[way])

    def stream(copy, landed, message, after):
        def step(j, send):
            for way in range(2):
                copy(way, j).wait_recv()
                if send:
                    shadow[way, Z + j] = landed[way, j]
                    ssend[way, j + U] = message(way, j + U)
                    copy(way, j + U).start()

        def batch(b, _):
            for t in range(B):
                step(b * B + t, True)
            after(b)
            return 0

        for j in range(U):
            for way in range(2):
                ssend[way, j] = message(way, j)
                copy(way, j).start()
        whole = (M - U) // B
        lax.fori_loop(0, whole, batch, 0)
        for b in range(whole, M // B):
            for t in range(B):
                step(b * B + t, b * B + t + U < M)
            after(b)

    def reduced(way, j):
        own = sb[way, rs_ref[way * M + j]]
        came = shadow[way, Z + j - lag_ref[way]]
        return own + came

    stream(s_copy, srecv, reduced, lambda b: None)
    for way in range(2):
        remote(ssend.at[way], srecv.at[way], s_send.at[way], s_recv.at[way, 0], z_to[way]).wait_send()

    def final(way, place, i):
        came = srecv[way, fin_ref[way * 2 * CAP + place] + i].astype(F32)
        own = sb[way, kslot_ref[place] * Q + i].astype(F32)
        return (came + own).astype(BF16)

    def gx_copy(s):
        return remote(gx.at[s], gfull.at[s, core], gx_send.at[s], gx_recv.at[s], peer)

    def gx_arrive(s):
        return remote(gx.at[s], gfull.at[s, mate], gx_send.at[s], gx_recv.at[s], peer)

    for s in range(CAP):
        for way in range(2):
            for i in range(Q):
                gx[s, way * Q + i] = final(way, mate * CAP + s, i)
        gx_copy(s).start()
    for s in range(CAP):
        for way in range(2):
            for i in range(Q):
                gfull[s, core, way * Q + i] = final(way, core * CAP + s, i)

    def o_copy(s):
        place = core * CAP + s
        return remote(res.at[s, mate], own4.at[:, pl.ds(place * Q, Q)], o_send.at[s], o_recv.at[s], peer)

    def o_arrive(s):
        place = mate * CAP + s
        return remote(res.at[s, mate], own4.at[:, pl.ds(place * Q, Q)], o_send.at[s], o_recv.at[s], peer)

    for s in range(CAP):
        gx_arrive(s).wait_recv()
        g = gfull[s].reshape(BLOCK, BLOCK)
        gram = mm_t(g, g).astype(BF16)
        cube = mm(g, gram).astype(BF16)
        m = mm(ops[s, 0], g) + mm(ops[s, 1], g) - mm(ops[s, 2], cube)
        n = cf[s] - mm(ops[s, 3], gram)
        p = mm(m.astype(BF16), n.astype(BF16))
        inv = lax.rsqrt(jnp.sum(p * p, keepdims=True) * (1.0 / (BLOCK * BLOCK)) + 1e-06)
        res[s] = (p * inv).astype(BF16).reshape(2, 2, Q, ROWS, BLOCK)
        o_copy(s).start()
        own4[:, pl.ds((core * CAP + s) * Q, Q)] = res[s, core]

    def handed(src, count, first, half):
        return [src, out.at[half, :, pl.ds(first, count)]]

    def f_here(b):
        src, dst = handed(arecv.at[:, pl.ds(b * B, B)], B, b * B, core)
        return pltpu.make_async_copy(src, dst, f_local.at[0])

    def f_mate(b):
        src, dst = handed(arecv.at[:, pl.ds(b * B, B)], B, b * B, core)
        return remote(src, dst, f_send.at[0], f_recv.at[0], peer)

    def spread(b):
        f_here(b).start()
        f_mate(b).start()

    for s in range(CAP):
        o_arrive(s).wait_recv()
    for way in range(2):
        for i in range(Z):
            shadow[way, i] = own4[way, ag_ref[i]]
    src, dst = handed(own4, 2 * CAP * Q, M, core)
    t_here = pltpu.make_async_copy(src, dst, t_local.at[0])
    t_mate = remote(src, dst, t_send.at[0], t_recv.at[0], peer)
    t_here.start()
    t_mate.start()

    stream(a_copy, arecv, lambda way, j: shadow[way, Z + j - lag_ref[2]], spread)

    for way in range(2):
        remote(ssend.at[way], arecv.at[way], a_send.at[way], a_recv.at[way, 0], z_to[way]).wait_send()
    src, dst = handed(arecv, M, 0, core)
    pltpu.make_async_copy(src, dst, f_local.at[0]).wait()
    remote(src, dst, f_send.at[0], f_recv.at[0], peer).wait_send()
    src, dst = handed(arecv, M, 0, mate)
    remote(src, dst, f_send.at[0], f_recv.at[0], peer).wait_recv()
    t_here.wait()
    t_mate.wait_send()
    src, dst = handed(own4, 2 * CAP * Q, M, mate)
    remote(src, dst, t_send.at[0], t_recv.at[0], peer).wait_recv()
    for buf, send, to in ((hb, x_send, x_to), (gb, y_send, y_to)):
        sent = buf.at[:, pl.ds(0, 3 * TOK)]
        remote(sent, sent, send.at[0], send.at[0], to[0]).wait_send()
    remote(pb.at[:, mate], eb, pe_send.at[0], pe_recv.at[0], peer).wait_send()
    for s in range(CAP):
        gx_copy(s).wait_send()
        o_copy(s).wait_send()


def run_main(owners, hidden, grad_out, left_stat, right_stat, left_root, right_root):
    dma = pltpu.SemaphoreType.DMA
    anywhere = pl.BlockSpec(memory_space=pl.ANY)
    scalars = pl.BlockSpec(memory_space=pltpu.SMEM)
    stream = pltpu.VMEM((2, M, ROWS, BLOCK), BF16)

    def table(size):
        return pltpu.SMEM((size,), jnp.int32)

    return pl.pallas_call(
        main_kernel,
        out_shape=(
            jax.ShapeDtypeStruct((2, 2, M + 2 * CAP * Q, ROWS, BLOCK), BF16),
            jax.ShapeDtypeStruct((2 * NB,), jnp.int32),
        ),
        in_specs=[scalars] + [anywhere] * 6,
        out_specs=(anywhere, scalars),
        scratch_shapes=[
            pltpu.VMEM((BR, 4 * TOK, BLOCK), BF16),
            pltpu.VMEM((BC, 4 * TOK, BLOCK), BF16),
            pltpu.VMEM((NB, 2, 2 * Q, ROWS, BLOCK), BF16),
            pltpu.VMEM((NB, 2 * Q, ROWS, BLOCK), BF16),
            pltpu.VMEM((2, NB * Q, ROWS, BLOCK), BF16),
            stream,
            stream,
            stream,
            pltpu.VMEM((2, Z + M, ROWS, BLOCK), BF16),
            pltpu.VMEM((CAP, 2, 2 * Q, ROWS, BLOCK), BF16),
            pltpu.VMEM((CAP, 2 * Q, ROWS, BLOCK), BF16),
            pltpu.VMEM((2, 2 * CAP * Q, ROWS, BLOCK), BF16),
            pltpu.VMEM((CAP, 2, 2, Q, ROWS, BLOCK), BF16),
            pltpu.VMEM((4, CAP, BLOCK, BLOCK), BF16),
            pltpu.VMEM((CAP, 4, BLOCK, BLOCK), BF16),
            pltpu.VMEM((CAP, BLOCK, BLOCK), F32),
            table(CHIPS), table(CHIPS), table(2 * M), table(4 * CAP), table(2 * CAP), table(Z), table(3),
            dma((11,)),
            dma((1,)), dma((BR, 4)), dma((1,)), dma((BC, 4)),
            dma((1,)), dma((NB,)),
            dma((2,)), dma((2, M)), dma((2,)), dma((2, M)),
            dma((CAP,)), dma((CAP,)), dma((CAP,)), dma((CAP,)),
            dma((1,)), dma((1,)), dma((1,)),
            dma((1,)), dma((1,)), dma((1,)),
        ],
        compiler_params=pltpu.CompilerParams(
            collective_id=0, has_side_effects=True, vmem_limit_bytes=62 * 1024 * 1024
        ),
        name="main",
    )(owners, hidden, grad_out, left_stat, right_stat, left_root, right_root)


def lay_out_kernel(pos, pieces, out, buf, in_sem, out_sem):
    def reads(k):
        return [
            pltpu.make_async_copy(
                pieces.at[half, way, pl.ds(pos[way * NB + k], Q)], buf.at[k, half, way], in_sem.at[k, half, way]
            )
            for half in range(2)
            for way in range(2)
        ]

    def write(k):
        r, c = k // BC, k % BC
        return pltpu.make_async_copy(
            buf.at[k].reshape(BLOCK, BLOCK),
            out.at[pl.ds(r * BLOCK, BLOCK), pl.ds(c * BLOCK, BLOCK)],
            out_sem.at[k],
        )

    for k in range(NB):
        for copy in reads(k):
            copy.start()
    for k in range(NB):
        for copy in reads(k):
            copy.wait()
        write(k).start()
    for k in range(NB):
        write(k).wait()


def run_lay_out(pos, pieces):
    dma = pltpu.SemaphoreType.DMA
    return pl.pallas_call(
        lay_out_kernel,
        out_shape=jax.ShapeDtypeStruct((BR * BLOCK, BC * BLOCK), BF16),
        in_specs=[pl.BlockSpec(memory_space=pltpu.SMEM), pl.BlockSpec(memory_space=pl.ANY)],
        out_specs=pl.BlockSpec(memory_space=pl.ANY),
        scratch_shapes=[
            pltpu.VMEM((NB, 2, 2, Q, ROWS, BLOCK), BF16),
            dma((NB, 2, 2)),
            dma((NB,)),
        ],
        compiler_params=pltpu.CompilerParams(vmem_limit_bytes=60 * 1024 * 1024),
        name="lay_out",
    )(pos, pieces)


def shards(hidden, grad_out, block_owner, left_stat, right_stat, left_root, right_root):
    pieces, pos = run_main(
        block_owner.reshape(NB), hidden, grad_out, left_stat, right_stat, left_root, right_root
    )
    return run_lay_out(pos, pieces)


def solution(mesh):
    in_specs = (
        P(("dp", "pre"), "mp"),
        P(("dp", "mp"), "pre"),
        P("mp", "pre", None, None),
        P("dp", "mp", "pre"),
        P("dp", "mp", "pre"),
        P("dp", "mp", "pre"),
        P("dp", "mp", "pre"),
    )
    return jax.shard_map(
        shards, mesh=mesh, in_specs=in_specs, out_specs=P("mp", "pre"), check_vma=False
    )
```

```python
import jax
import jax.numpy as jnp
from jax import lax
from jax.experimental import pallas as pl
from jax.experimental.pallas import tpu as pltpu
from jax.sharding import PartitionSpec as P

MESH = pl.DeviceIdType.MESH
F32 = jnp.float32
BF16 = jnp.bfloat16

BLOCK = 512
BR = 3
BC = 4
NB = BR * BC
CAP = 2
CHIPS = 8
TOK = 256

Q = 4
U = 5
ROWS = BLOCK // 4 // Q
Z = max(2 * CAP * Q, U)
M = NB * Q + 4 * U
B = 4
assert M % B == 0 and Q * 2 >= U


def split(value):
    high = value.astype(BF16)
    return high, (value - high.astype(F32)).astype(BF16)


def mm(a, b):
    return jnp.dot(a, b, preferred_element_type=F32)


def mm_t(a, b):
    return lax.dot_general(a, b, (((0,), (0,)), ((), ())), preferred_element_type=F32)


def fifth(x, stat):
    sh, sl = split(mm(x, x))
    qh, ql = split(mm(sh, sh) + mm(sh, sl) + mm(sl, sh))
    x5 = mm(qh, x) + mm(ql, x)
    h, low = split(x5)
    return 1.25 * x.astype(F32) - 0.2 * (mm(h, stat) + mm(low, stat)), 0.05 * x5


def total(terms):
    result = terms[0]
    for term in terms[1:]:
        result = result + term
    return result


def make_tables(owner_ref, chip, places_ref, before_ref, rs_ref, fin_ref, kslot_ref, ag_ref, lag_ref, pos_ref):
    i32 = jnp.int32
    owner = [owner_ref[k] for k in range(NB)]
    dest = [lax.div(o, 2) for o in owner]

    def ones(flags):
        return total([f.astype(i32) for f in flags]) if flags else jnp.int32(0)

    slot = [jnp.minimum(ones([owner[e] == owner[k] for e in range(k)]), CAP - 1) for k in range(NB)]
    rank = [jnp.minimum(ones([dest[e] == dest[k] for e in range(k)]), 2 * CAP - 1) for k in range(NB)]
    local = [lax.rem(owner[k], 2) * CAP + slot[k] for k in range(NB)]
    for d in range(CHIPS):
        places_ref[d] = jnp.clip(ones([dest[k] == d for k in range(NB)]) * Q, U, Z)
    mine = places_ref[chip]
    lag_ref[2] = mine
    here = [(dest[k] == chip).astype(i32) for k in range(NB)]
    for s in range(2 * CAP):
        kslot_ref[s] = jnp.minimum(
            total([here[k] * (local[k] == s).astype(i32) * k for k in range(NB)]), NB - 1
        )
    for way, sigma in enumerate((1, -1)):
        near = [places_ref[lax.rem(chip + CHIPS - g * sigma, CHIPS)] for g in range(CHIPS)]
        lag_ref[way] = near[1]
        running = jnp.int32(0)
        for g in range(1, CHIPS):
            before_ref[g] = running
            running = running + near[g]
        before_ref[0] = running
        spot = []
        for k in range(NB):
            gap = lax.rem((chip - dest[k]) * sigma + CHIPS, CHIPS)
            spot.append(before_ref[gap] + rank[k] * Q)
            pos_ref[way * NB + k] = jnp.where(here[k] == 1, M + local[k] * Q, jnp.minimum(spot[k], M - Q))
        for s in range(2 * CAP):
            last = total(
                [here[k] * (local[k] == s).astype(i32) * (running - near[1] + rank[k] * Q) for k in range(NB)]
            )
            fin_ref[way * 2 * CAP + s] = jnp.minimum(last, M - Q)

        def piece_of(j, _):
            codes = []
            for k in range(NB):
                off = j - spot[k]
                codes.append(jnp.where((off >= 0) & (off < Q), k * Q + off, 0))
            rs_ref[way * M + j] = jnp.minimum(total(codes), NB * Q - 1)
            return 0

        lax.fori_loop(0, M, piece_of, 0)
    for i in range(Z):
        codes = []
        for k in range(NB):
            off = i - Z + mine - rank[k] * Q
            codes.append(jnp.where((here[k] == 1) & (off >= 0) & (off < Q), local[k] * Q + off, 0))
        ag_ref[i] = jnp.minimum(total(codes), 2 * CAP * Q - 1)


def main_kernel(
    owner_ref, hid, gro, ls, rs, lr, rr, out, pos_ref,
    hb, gb, pb, eb, sb, ssend, srecv, arecv, shadow, gfull, gx, own4, res, stats, ops, cf, acc,
    places_ref, before_ref, rs_ref, fin_ref, kslot_ref, ag_ref, lag_ref,
    local_sem, x_send, x_recv, y_send, y_recv, pe_send, pe_recv,
    s_send, s_recv, a_send, a_recv, gx_send, gx_recv, o_send, o_recv,
    f_local, f_send, f_recv, t_local, t_send, t_recv,
):
    dp = lax.axis_index("dp")
    mp = lax.axis_index("mp")
    pre = lax.axis_index("pre")
    chip = dp // 2
    core = lax.rem(dp, 2)
    mate = 1 - core
    peer = {"dp": chip * 2 + mate}
    x_to = [{"pre": lax.rem(pre + 1, 4)}, {"pre": lax.rem(pre + 3, 4)}]
    y_to = [{"mp": lax.rem(mp + 1, 4)}, {"mp": lax.rem(mp + 3, 4)}]
    z_to = [
        {"dp": lax.rem(chip + 1, CHIPS) * 2 + core},
        {"dp": lax.rem(chip + CHIPS - 1, CHIPS) * 2 + core},
    ]

    def remote(src, dst, send, recv, to):
        return pltpu.make_async_remote_copy(
            src_ref=src, dst_ref=dst, send_sem=send, recv_sem=recv, device_id=to, device_id_type=MESH
        )

    stat_copies = [
        pltpu.make_async_copy(src, stats.at[i], local_sem.at[i]) for i, src in enumerate((ls, rs, lr, rr))
    ]
    token_copies = []
    for i in range(BC):
        if i < BR:
            token_copies.append(
                pltpu.make_async_copy(
                    hid.at[:, pl.ds(i * BLOCK, BLOCK)], hb.at[i, pl.ds(pre * TOK, TOK)], local_sem.at[4 + i]
                )
            )
        token_copies.append(
            pltpu.make_async_copy(
                gro.at[:, pl.ds(i * BLOCK, BLOCK)], gb.at[i, pl.ds(mp * TOK, TOK)], local_sem.at[7 + i]
            )
        )
    for copy in token_copies + stat_copies:
        copy.start()

    barrier = pltpu.get_barrier_semaphore()
    for to in [peer] + x_to + y_to + z_to:
        pl.semaphore_signal(barrier, inc=1, device_id=to, device_id_type=MESH)
    pl.semaphore_wait(barrier, 7)

    def gather(src, buf, me, to, send, recv):
        def direct(i, way):
            return remote(
                src.at[:, pl.ds(i * BLOCK, BLOCK)],
                buf.at[i, pl.ds(me * TOK, TOK)],
                send.at[0], recv.at[i, way], to[way],
            )

        def arrived(i, way):
            who = lax.rem(me + (3 if way == 0 else 1), 4)
            part = buf.at[i, pl.ds(who * TOK, TOK)]
            return remote(part, part, send.at[0], recv.at[i, way], to[way])

        def forward(i, way):
            who = lax.rem(me + (3 if way == 0 else 1), 4)
            part = buf.at[i, pl.ds(who * TOK + way * (TOK // 2), TOK // 2)]
            return remote(part, part, send.at[0], recv.at[i, 2 + way], to[way])

        def far(i, way):
            who = lax.rem(me + 2, 4)
            part = buf.at[i, pl.ds(who * TOK + way * (TOK // 2), TOK // 2)]
            return remote(part, part, send.at[0], recv.at[i, 2 + way], to[way])

        return direct, arrived, forward, far

    rings = [
        (BR, gather(hid, hb, pre, x_to, x_send, x_recv)),
        (BC, gather(gro, gb, mp, y_to, y_send, y_recv)),
    ]

    def start_direct(i):
        for count, (direct, _, _, _) in rings:
            if i < count:
                for way in range(2):
                    direct(i, way).start()

    def pass_on(i):
        for count, (_, arrived, forward, _) in rings:
            if i < count:
                for way in range(2):
                    arrived(i, way).wait_recv()
                    forward(i, way).start()

    def finish(i, which):
        count, (_, _, _, far) = rings[which]
        if i < count:
            for way in range(2):
                far(i, way).wait_recv()

    def operators(side, s):
        a, b = fifth(stats[2 + side, s], stats[side, s])
        if side == 0:
            ops[s, 0], ops[s, 1] = split(a)
            ops[s, 2] = b.astype(BF16)
        else:
            cf[s] = a
            ops[s, 3] = b.astype(BF16)

    def to_mate(k):
        return remote(pb.at[k, mate], eb.at[k], pe_send.at[0], pe_recv.at[k], peer)

    def store(k, value):
        pb[k] = value.astype(BF16).reshape(2, 2 * Q, ROWS, BLOCK)
        to_mate(k).start()

    def partial(r, c):
        store(r * BC + c, mm_t(hb[r], gb[c]))

    def part(r, c, step):
        rows = pl.ds(lax.rem(mp + step, 4) * TOK, TOK)
        return mm_t(hb[r, rows], gb[c, rows])

    def early(r, c):
        acc[r] = part(r, c, 0) + part(r, c, 1) + part(r, c, 3)

    def late(r, c):
        store(r * BC + c, acc[r] + part(r, c, 2))

    def add_halves(r, c):
        k = r * BC + c
        to_mate(k).wait_recv()
        for way in range(2):
            both = pb[k, core, pl.ds(way * Q, Q)].astype(F32) + eb[k, pl.ds(way * Q, Q)].astype(F32)
            sb[way, pl.ds(k * Q, Q)] = both.astype(BF16)

    def rows_of(c, what, count=BR):
        lax.fori_loop(0, count, lambda r, _: (what(r, c), 0)[1], 0)

    start_direct(0)
    start_direct(1)
    for copy in token_copies + stat_copies:
        copy.wait()
    operators(0, 0)
    operators(1, 0)
    pass_on(0)
    start_direct(2)
    operators(0, 1)
    for way in range(2):
        shadow[way, pl.ds(0, Z)] = jnp.zeros((Z, ROWS, BLOCK), BF16)
    pass_on(1)
    start_direct(3)
    operators(1, 1)
    finish(0, 0)
    finish(0, 1)
    partial(0, 0)
    make_tables(
        owner_ref, chip, places_ref, before_ref, rs_ref, fin_ref, kslot_ref, ag_ref, lag_ref, pos_ref
    )
    pass_on(2)
    finish(1, 0)
    finish(1, 1)
    rows_of(1, partial, 2)
    partial(1, 0)
    finish(2, 0)
    lax.fori_loop(0, 2, lambda c, _: (partial(2, c), 0)[1], 0)
    pass_on(3)
    rows_of(2, early)
    finish(2, 1)
    rows_of(2, late)
    rows_of(3, early)
    for c in range(2):
        rows_of(c, add_halves)
    finish(3, 1)
    rows_of(3, late)
    for c in range(2, BC):
        rows_of(c, add_halves)

    def s_copy(way, j):
        return remote(ssend.at[way, j], srecv.at[way, j], s_send.at[way], s_recv.at[way, j], z_to[way])

    def a_copy(way, j):
        return remote(ssend.at[way, j], arecv.at[way, j], a_send.at[way], a_recv.at[way, j], z_to[way])

    def stream(copy, landed, message, after):
        def step(j, send):
            for way in range(2):
                copy(way, j).wait_recv()
                if send:
                    shadow[way, Z + j] = landed[way, j]
                    ssend[way, j + U] = message(way, j + U)
                    copy(way, j + U).start()

        def batch(b, _):
            for t in range(B):
                step(b * B + t, True)
            after(b)
            return 0

        for j in range(U):
            for way in range(2):
                ssend[way, j] = message(way, j)
                copy(way, j).start()
        whole = (M - U) // B
        lax.fori_loop(0, whole, batch, 0)
        for b in range(whole, M // B):
            for t in range(B):
                step(b * B + t, b * B + t + U < M)
            after(b)

    def reduced(way, j):
        own = sb[way, rs_ref[way * M + j]]
        came = shadow[way, Z + j - lag_ref[way]]
        return own + came

    stream(s_copy, srecv, reduced, lambda b: None)
    for way in range(2):
        remote(ssend.at[way], srecv.at[way], s_send.at[way], s_recv.at[way, 0], z_to[way]).wait_send()

    def final(way, place, i):
        came = srecv[way, fin_ref[way * 2 * CAP + place] + i].astype(F32)
        own = sb[way, kslot_ref[place] * Q + i].astype(F32)
        return (came + own).astype(BF16)

    def gx_copy(s):
        return remote(gx.at[s], gfull.at[s, core], gx_send.at[s], gx_recv.at[s], peer)

    def gx_arrive(s):
        return remote(gx.at[s], gfull.at[s, mate], gx_send.at[s], gx_recv.at[s], peer)

    for s in range(CAP):
        for way in range(2):
            for i in range(Q):
                gx[s, way * Q + i] = final(way, mate * CAP + s, i)
        gx_copy(s).start()
    for s in range(CAP):
        for way in range(2):
            for i in range(Q):
                gfull[s, core, way * Q + i] = final(way, core * CAP + s, i)

    def o_copy(s):
        place = core * CAP + s
        return remote(res.at[s, mate], own4.at[:, pl.ds(place * Q, Q)], o_send.at[s], o_recv.at[s], peer)

    def o_arrive(s):
        place = mate * CAP + s
        return remote(res.at[s, mate], own4.at[:, pl.ds(place * Q, Q)], o_send.at[s], o_recv.at[s], peer)

    both = range(CAP)
    for s in both:
        gx_arrive(s).wait_recv()
    g = [gfull[s].reshape(BLOCK, BLOCK) for s in both]
    gram = [mm_t(g[s], g[s]).astype(BF16) for s in both]
    cube = [mm(g[s], gram[s]).astype(BF16) for s in both]
    m = [(mm(ops[s, 0], g[s]) + mm(ops[s, 1], g[s]) - mm(ops[s, 2], cube[s])).astype(BF16) for s in both]
    n = [(cf[s] - mm(ops[s, 3], gram[s])).astype(BF16) for s in both]
    for s in both:
        p = mm(m[s], n[s])
        inv = lax.rsqrt(jnp.sum(p * p, keepdims=True) * (1.0 / (BLOCK * BLOCK)) + 1e-06)
        res[s] = (p * inv).astype(BF16).reshape(2, 2, Q, ROWS, BLOCK)
        o_copy(s).start()
        own4[:, pl.ds((core * CAP + s) * Q, Q)] = res[s, core]

    def handed(src, count, first, half):
        return [src, out.at[half, :, pl.ds(first, count)]]

    def f_here(b):
        src, dst = handed(arecv.at[:, pl.ds(b * B, B)], B, b * B, core)
        return pltpu.make_async_copy(src, dst, f_local.at[0])

    def f_mate(b):
        src, dst = handed(arecv.at[:, pl.ds(b * B, B)], B, b * B, core)
        return remote(src, dst, f_send.at[0], f_recv.at[0], peer)

    def spread(b):
        f_here(b).start()
        f_mate(b).start()

    for s in range(CAP):
        o_arrive(s).wait_recv()
    for way in range(2):
        for i in range(Z):
            shadow[way, i] = own4[way, ag_ref[i]]
    src, dst = handed(own4, 2 * CAP * Q, M, core)
    t_here = pltpu.make_async_copy(src, dst, t_local.at[0])
    t_mate = remote(src, dst, t_send.at[0], t_recv.at[0], peer)
    t_here.start()
    t_mate.start()

    stream(a_copy, arecv, lambda way, j: shadow[way, Z + j - lag_ref[2]], spread)

    for way in range(2):
        remote(ssend.at[way], arecv.at[way], a_send.at[way], a_recv.at[way, 0], z_to[way]).wait_send()
    src, dst = handed(arecv, M, 0, core)
    pltpu.make_async_copy(src, dst, f_local.at[0]).wait()
    remote(src, dst, f_send.at[0], f_recv.at[0], peer).wait_send()
    src, dst = handed(arecv, M, 0, mate)
    remote(src, dst, f_send.at[0], f_recv.at[0], peer).wait_recv()
    t_here.wait()
    t_mate.wait_send()
    src, dst = handed(own4, 2 * CAP * Q, M, mate)
    remote(src, dst, t_send.at[0], t_recv.at[0], peer).wait_recv()
    for buf, send, to in ((hb, x_send, x_to), (gb, y_send, y_to)):
        sent = buf.at[:, pl.ds(0, 3 * TOK)]
        remote(sent, sent, send.at[0], send.at[0], to[0]).wait_send()
    remote(pb.at[:, mate], eb, pe_send.at[0], pe_recv.at[0], peer).wait_send()
    for s in range(CAP):
        gx_copy(s).wait_send()
        o_copy(s).wait_send()


def run_main(owners, hidden, grad_out, left_stat, right_stat, left_root, right_root):
    dma = pltpu.SemaphoreType.DMA
    anywhere = pl.BlockSpec(memory_space=pl.ANY)
    scalars = pl.BlockSpec(memory_space=pltpu.SMEM)
    stream = pltpu.VMEM((2, M, ROWS, BLOCK), BF16)

    def table(size):
        return pltpu.SMEM((size,), jnp.int32)

    return pl.pallas_call(
        main_kernel,
        out_shape=(
            jax.ShapeDtypeStruct((2, 2, M + 2 * CAP * Q, ROWS, BLOCK), BF16),
            jax.ShapeDtypeStruct((2 * NB,), jnp.int32),
        ),
        in_specs=[scalars] + [anywhere] * 6,
        out_specs=(anywhere, scalars),
        scratch_shapes=[
            pltpu.VMEM((BR, 4 * TOK, BLOCK), BF16),
            pltpu.VMEM((BC, 4 * TOK, BLOCK), BF16),
            pltpu.VMEM((NB, 2, 2 * Q, ROWS, BLOCK), BF16),
            pltpu.VMEM((NB, 2 * Q, ROWS, BLOCK), BF16),
            pltpu.VMEM((2, NB * Q, ROWS, BLOCK), BF16),
            stream,
            stream,
            stream,
            pltpu.VMEM((2, Z + M, ROWS, BLOCK), BF16),
            pltpu.VMEM((CAP, 2, 2 * Q, ROWS, BLOCK), BF16),
            pltpu.VMEM((CAP, 2 * Q, ROWS, BLOCK), BF16),
            pltpu.VMEM((2, 2 * CAP * Q, ROWS, BLOCK), BF16),
            pltpu.VMEM((CAP, 2, 2, Q, ROWS, BLOCK), BF16),
            pltpu.VMEM((4, CAP, BLOCK, BLOCK), BF16),
            pltpu.VMEM((CAP, 4, BLOCK, BLOCK), BF16),
            pltpu.VMEM((CAP, BLOCK, BLOCK), F32),
            pltpu.VMEM((BR, BLOCK, BLOCK), F32),
            table(CHIPS), table(CHIPS), table(2 * M), table(4 * CAP), table(2 * CAP), table(Z), table(3),
            dma((11,)),
            dma((1,)), dma((BR, 4)), dma((1,)), dma((BC, 4)),
            dma((1,)), dma((NB,)),
            dma((2,)), dma((2, M)), dma((2,)), dma((2, M)),
            dma((CAP,)), dma((CAP,)), dma((CAP,)), dma((CAP,)),
            dma((1,)), dma((1,)), dma((1,)),
            dma((1,)), dma((1,)), dma((1,)),
        ],
        compiler_params=pltpu.CompilerParams(
            collective_id=0, has_side_effects=True, vmem_limit_bytes=62 * 1024 * 1024
        ),
        name="main",
    )(owners, hidden, grad_out, left_stat, right_stat, left_root, right_root)


def lay_out_kernel(pos, pieces, out, buf, in_sem, out_sem):
    def reads(k):
        return [
            pltpu.make_async_copy(
                pieces.at[half, way, pl.ds(pos[way * NB + k], Q)], buf.at[k, half, way], in_sem.at[k, half, way]
            )
            for half in range(2)
            for way in range(2)
        ]

    def write(k):
        r, c = k // BC, k % BC
        return pltpu.make_async_copy(
            buf.at[k].reshape(BLOCK, BLOCK),
            out.at[pl.ds(r * BLOCK, BLOCK), pl.ds(c * BLOCK, BLOCK)],
            out_sem.at[k],
        )

    for k in range(NB):
        for copy in reads(k):
            copy.start()
    for k in range(NB):
        for copy in reads(k):
            copy.wait()
        write(k).start()
    for k in range(NB):
        write(k).wait()


def run_lay_out(pos, pieces):
    dma = pltpu.SemaphoreType.DMA
    return pl.pallas_call(
        lay_out_kernel,
        out_shape=jax.ShapeDtypeStruct((BR * BLOCK, BC * BLOCK), BF16),
        in_specs=[pl.BlockSpec(memory_space=pltpu.SMEM), pl.BlockSpec(memory_space=pl.ANY)],
        out_specs=pl.BlockSpec(memory_space=pl.ANY),
        scratch_shapes=[
            pltpu.VMEM((NB, 2, 2, Q, ROWS, BLOCK), BF16),
            dma((NB, 2, 2)),
            dma((NB,)),
        ],
        compiler_params=pltpu.CompilerParams(vmem_limit_bytes=60 * 1024 * 1024),
        name="lay_out",
    )(pos, pieces)


def shards(hidden, grad_out, block_owner, left_stat, right_stat, left_root, right_root):
    pieces, pos = run_main(
        block_owner.reshape(NB), hidden, grad_out, left_stat, right_stat, left_root, right_root
    )
    return run_lay_out(pos, pieces)


def solution(mesh):
    in_specs = (
        P(("dp", "pre"), "mp"),
        P(("dp", "mp"), "pre"),
        P("mp", "pre", None, None),
        P("dp", "mp", "pre"),
        P("dp", "mp", "pre"),
        P("dp", "mp", "pre"),
        P("dp", "mp", "pre"),
    )
    return jax.shard_map(
        shards, mesh=mesh, in_specs=in_specs, out_specs=P("mp", "pre"), check_vma=False
    )
```

```python
import jax
import jax.numpy as jnp
from jax import lax
from jax.experimental import pallas as pl
from jax.experimental.pallas import tpu as pltpu
from jax.sharding import PartitionSpec as P

MESH = pl.DeviceIdType.MESH
F32 = jnp.float32
BF16 = jnp.bfloat16

BLOCK = 512
BR = 3
BC = 4
NB = BR * BC
CAP = 2
CHIPS = 8
TOK = 256

Q = 4
U = 5
ROWS = BLOCK // 4 // Q
Z = max(2 * CAP * Q, U)
M = NB * Q + 4 * U
R = min(M, CHIPS * U)
B = 4
assert M % B == 0 and Q * 2 >= U


def split(value):
    high = value.astype(BF16)
    return high, (value - high.astype(F32)).astype(BF16)


def mm(a, b):
    return jnp.dot(a, b, preferred_element_type=F32)


def mm_t(a, b):
    return lax.dot_general(a, b, (((0,), (0,)), ((), ())), preferred_element_type=F32)


def fifth(x, stat):
    sh, sl = split(mm(x, x))
    qh, ql = split(mm(sh, sh) + mm(sh, sl) + mm(sl, sh))
    x5 = mm(qh, x) + mm(ql, x)
    h, low = split(x5)
    return 1.25 * x.astype(F32) - 0.2 * (mm(h, stat) + mm(low, stat)), 0.05 * x5


def total(terms):
    result = terms[0]
    for term in terms[1:]:
        result = result + term
    return result


def make_tables(owner_ref, chip, places_ref, before_ref, rs_ref, fin_ref, kslot_ref, ag_ref, lag_ref, pos_ref):
    i32 = jnp.int32
    owner = [owner_ref[k] for k in range(NB)]
    dest = [lax.div(o, 2) for o in owner]

    def ones(flags):
        return total([f.astype(i32) for f in flags]) if flags else jnp.int32(0)

    slot = [jnp.minimum(ones([owner[e] == owner[k] for e in range(k)]), CAP - 1) for k in range(NB)]
    rank = [jnp.minimum(ones([dest[e] == dest[k] for e in range(k)]), 2 * CAP - 1) for k in range(NB)]
    local = [lax.rem(owner[k], 2) * CAP + slot[k] for k in range(NB)]
    for d in range(CHIPS):
        places_ref[d] = jnp.clip(ones([dest[k] == d for k in range(NB)]) * Q, U, Z)
    mine = places_ref[chip]
    lag_ref[2] = mine
    here = [(dest[k] == chip).astype(i32) for k in range(NB)]
    for s in range(2 * CAP):
        kslot_ref[s] = jnp.minimum(
            total([here[k] * (local[k] == s).astype(i32) * k for k in range(NB)]), NB - 1
        )
    for way, sigma in enumerate((1, -1)):
        near = [places_ref[lax.rem(chip + CHIPS - g * sigma, CHIPS)] for g in range(CHIPS)]
        lag_ref[way] = near[1]
        running = jnp.int32(0)
        for g in range(1, CHIPS):
            before_ref[g] = running
            running = running + near[g]
        before_ref[0] = running
        spot = []
        for k in range(NB):
            gap = lax.rem((chip - dest[k]) * sigma + CHIPS, CHIPS)
            spot.append(before_ref[gap] + rank[k] * Q)
            pos_ref[way * NB + k] = jnp.where(here[k] == 1, M + local[k] * Q, jnp.minimum(spot[k], M - Q))
        for s in range(2 * CAP):
            last = total(
                [here[k] * (local[k] == s).astype(i32) * (running - near[1] + rank[k] * Q) for k in range(NB)]
            )
            fin_ref[way * 2 * CAP + s] = jnp.minimum(last, M - Q)

        def piece_of(j, _):
            codes = []
            for k in range(NB):
                off = j - spot[k]
                codes.append(jnp.where((off >= 0) & (off < Q), k * Q + off, 0))
            rs_ref[way * M + j] = jnp.minimum(total(codes), NB * Q - 1)
            return 0

        lax.fori_loop(0, M, piece_of, 0)
    for i in range(Z):
        codes = []
        for k in range(NB):
            off = i - Z + mine - rank[k] * Q
            codes.append(jnp.where((here[k] == 1) & (off >= 0) & (off < Q), local[k] * Q + off, 0))
        ag_ref[i] = jnp.minimum(total(codes), 2 * CAP * Q - 1)


def main_kernel(
    owner_ref, hid, gro, ls, rs, lr, rr, out, pos_ref,
    hb, gb, pb, eb, sb, ssend, srecv, arecv, shadow, gfull, gx, own4, res, stats, ops, cf, acc,
    places_ref, before_ref, rs_ref, fin_ref, kslot_ref, ag_ref, lag_ref,
    local_sem, x_send, x_recv, y_send, y_recv, pe_send, pe_recv,
    s_send, s_recv, a_send, a_recv, gx_send, gx_recv, o_send, o_recv,
    f_local, f_send, f_recv, t_local, t_send, t_recv,
):
    dp = lax.axis_index("dp")
    mp = lax.axis_index("mp")
    pre = lax.axis_index("pre")
    chip = dp // 2
    core = lax.rem(dp, 2)
    mate = 1 - core
    peer = {"dp": chip * 2 + mate}
    x_to = [{"pre": lax.rem(pre + 1, 4)}, {"pre": lax.rem(pre + 3, 4)}]
    y_to = [{"mp": lax.rem(mp + 1, 4)}, {"mp": lax.rem(mp + 3, 4)}]
    z_to = [
        {"dp": lax.rem(chip + 1, CHIPS) * 2 + core},
        {"dp": lax.rem(chip + CHIPS - 1, CHIPS) * 2 + core},
    ]

    def remote(src, dst, send, recv, to):
        return pltpu.make_async_remote_copy(
            src_ref=src, dst_ref=dst, send_sem=send, recv_sem=recv, device_id=to, device_id_type=MESH
        )

    stat_copies = [
        pltpu.make_async_copy(src, stats.at[i], local_sem.at[i]) for i, src in enumerate((ls, rs, lr, rr))
    ]
    token_copies = []
    for i in range(BC):
        if i < BR:
            token_copies.append(
                pltpu.make_async_copy(
                    hid.at[:, pl.ds(i * BLOCK, BLOCK)], hb.at[i, pl.ds(pre * TOK, TOK)], local_sem.at[4 + i]
                )
            )
        token_copies.append(
            pltpu.make_async_copy(
                gro.at[:, pl.ds(i * BLOCK, BLOCK)], gb.at[i, pl.ds(mp * TOK, TOK)], local_sem.at[7 + i]
            )
        )
    for copy in token_copies + stat_copies:
        copy.start()

    barrier = pltpu.get_barrier_semaphore()
    for to in [peer] + x_to + y_to + z_to:
        pl.semaphore_signal(barrier, inc=1, device_id=to, device_id_type=MESH)
    pl.semaphore_wait(barrier, 7)

    def gather(src, buf, me, to, send, recv):
        def direct(i, way):
            return remote(
                src.at[:, pl.ds(i * BLOCK, BLOCK)],
                buf.at[i, pl.ds(me * TOK, TOK)],
                send.at[0], recv.at[i, way], to[way],
            )

        def arrived(i, way):
            who = lax.rem(me + (3 if way == 0 else 1), 4)
            part = buf.at[i, pl.ds(who * TOK, TOK)]
            return remote(part, part, send.at[0], recv.at[i, way], to[way])

        def forward(i, way):
            who = lax.rem(me + (3 if way == 0 else 1), 4)
            part = buf.at[i, pl.ds(who * TOK + way * (TOK // 2), TOK // 2)]
            return remote(part, part, send.at[0], recv.at[i, 2 + way], to[way])

        def far(i, way):
            who = lax.rem(me + 2, 4)
            part = buf.at[i, pl.ds(who * TOK + way * (TOK // 2), TOK // 2)]
            return remote(part, part, send.at[0], recv.at[i, 2 + way], to[way])

        return direct, arrived, forward, far

    rings = [
        (BR, gather(hid, hb, pre, x_to, x_send, x_recv)),
        (BC, gather(gro, gb, mp, y_to, y_send, y_recv)),
    ]

    def start_direct(i):
        for count, (direct, _, _, _) in rings:
            if i < count:
                for way in range(2):
                    direct(i, way).start()

    def pass_on(i):
        for count, (_, arrived, forward, _) in rings:
            if i < count:
                for way in range(2):
                    arrived(i, way).wait_recv()
                    forward(i, way).start()

    def finish(i, which):
        count, (_, _, _, far) = rings[which]
        if i < count:
            for way in range(2):
                far(i, way).wait_recv()

    def operators(side, s):
        a, b = fifth(stats[2 + side, s], stats[side, s])
        if side == 0:
            ops[s, 0], ops[s, 1] = split(a)
            ops[s, 2] = b.astype(BF16)
        else:
            cf[s] = a
            ops[s, 3] = b.astype(BF16)

    def to_mate(k):
        return remote(pb.at[k, mate], eb.at[k], pe_send.at[0], pe_recv.at[k], peer)

    def store(k, value):
        pb[k] = value.astype(BF16).reshape(2, 2 * Q, ROWS, BLOCK)
        to_mate(k).start()

    def partial(r, c):
        store(r * BC + c, mm_t(hb[r], gb[c]))

    def part(r, c, step):
        rows = pl.ds(lax.rem(mp + step, 4) * TOK, TOK)
        return mm_t(hb[r, rows], gb[c, rows])

    def early(r, c):
        acc[r] = part(r, c, 0) + part(r, c, 1) + part(r, c, 3)

    def late(r, c):
        store(r * BC + c, acc[r] + part(r, c, 2))

    def add_halves(r, c):
        k = r * BC + c
        to_mate(k).wait_recv()
        for way in range(2):
            both = pb[k, core, pl.ds(way * Q, Q)].astype(F32) + eb[k, pl.ds(way * Q, Q)].astype(F32)
            sb[way, pl.ds(k * Q, Q)] = both.astype(BF16)

    def rows_of(c, what, count=BR):
        lax.fori_loop(0, count, lambda r, _: (what(r, c), 0)[1], 0)

    start_direct(0)
    start_direct(1)
    for copy in token_copies + stat_copies:
        copy.wait()
    operators(0, 0)
    operators(1, 0)
    pass_on(0)
    start_direct(2)
    operators(0, 1)
    for way in range(2):
        shadow[way, pl.ds(0, Z)] = jnp.zeros((Z, ROWS, BLOCK), BF16)
    pass_on(1)
    start_direct(3)
    operators(1, 1)
    finish(0, 0)
    finish(0, 1)
    partial(0, 0)
    make_tables(
        owner_ref, chip, places_ref, before_ref, rs_ref, fin_ref, kslot_ref, ag_ref, lag_ref, pos_ref
    )
    pass_on(2)
    finish(1, 0)
    finish(1, 1)
    rows_of(1, partial, 2)
    partial(1, 0)
    finish(2, 0)
    lax.fori_loop(0, 2, lambda c, _: (partial(2, c), 0)[1], 0)
    pass_on(3)
    rows_of(2, early)
    finish(2, 1)
    rows_of(2, late)
    rows_of(3, early)
    for c in range(2):
        rows_of(c, add_halves)
    finish(3, 1)
    rows_of(3, late)
    for c in range(2, BC):
        rows_of(c, add_halves)

    def s_copy(way, j):
        return remote(ssend.at[way, j], srecv.at[way, j], s_send.at[way], s_recv.at[way, lax.rem(j, R)], z_to[way])

    def a_copy(way, j):
        return remote(ssend.at[way, j], arecv.at[way, j], a_send.at[way], a_recv.at[way, lax.rem(j, R)], z_to[way])

    def stream(copy, landed, message, after):
        def step(j, send):
            for way in range(2):
                copy(way, j).wait_recv()
                if send:
                    shadow[way, Z + j] = landed[way, j]
                    ssend[way, j + U] = message(way, j + U)
                    copy(way, j + U).start()

        def batch(b, _):
            for t in range(B):
                step(b * B + t, True)
            after(b)
            return 0

        for j in range(U):
            for way in range(2):
                ssend[way, j] = message(way, j)
                copy(way, j).start()
        whole = (M - U) // B
        lax.fori_loop(0, whole, batch, 0)
        for b in range(whole, M // B):
            for t in range(B):
                step(b * B + t, b * B + t + U < M)
            after(b)

    def reduced(way, j):
        own = sb[way, rs_ref[way * M + j]]
        came = shadow[way, Z + j - lag_ref[way]]
        return own + came

    stream(s_copy, srecv, reduced, lambda b: None)
    for way in range(2):
        remote(ssend.at[way], srecv.at[way], s_send.at[way], s_recv.at[way, 0], z_to[way]).wait_send()

    def final(way, place, i):
        came = srecv[way, fin_ref[way * 2 * CAP + place] + i].astype(F32)
        own = sb[way, kslot_ref[place] * Q + i].astype(F32)
        return (came + own).astype(BF16)

    def gx_copy(s):
        return remote(gx.at[s], gfull.at[s, core], gx_send.at[s], gx_recv.at[s], peer)

    def gx_arrive(s):
        return remote(gx.at[s], gfull.at[s, mate], gx_send.at[s], gx_recv.at[s], peer)

    for s in range(CAP):
        for way in range(2):
            for i in range(Q):
                gx[s, way * Q + i] = final(way, mate * CAP + s, i)
        gx_copy(s).start()
    for s in range(CAP):
        for way in range(2):
            for i in range(Q):
                gfull[s, core, way * Q + i] = final(way, core * CAP + s, i)

    def o_copy(s):
        place = core * CAP + s
        return remote(res.at[s, mate], own4.at[:, pl.ds(place * Q, Q)], o_send.at[s], o_recv.at[s], peer)

    def o_arrive(s):
        place = mate * CAP + s
        return remote(res.at[s, mate], own4.at[:, pl.ds(place * Q, Q)], o_send.at[s], o_recv.at[s], peer)

    both = range(CAP)
    for s in both:
        gx_arrive(s).wait_recv()
    g = [gfull[s].reshape(BLOCK, BLOCK) for s in both]
    gram = [mm_t(g[s], g[s]).astype(BF16) for s in both]
    cube = [mm(g[s], gram[s]).astype(BF16) for s in both]
    m = [(mm(ops[s, 0], g[s]) + mm(ops[s, 1], g[s]) - mm(ops[s, 2], cube[s])).astype(BF16) for s in both]
    n = [(cf[s] - mm(ops[s, 3], gram[s])).astype(BF16) for s in both]
    for s in both:
        p = mm(m[s], n[s])
        inv = lax.rsqrt(jnp.sum(p * p, keepdims=True) * (1.0 / (BLOCK * BLOCK)) + 1e-06)
        res[s] = (p * inv).astype(BF16).reshape(2, 2, Q, ROWS, BLOCK)
        o_copy(s).start()
        own4[:, pl.ds((core * CAP + s) * Q, Q)] = res[s, core]

    def handed(src, count, first, half):
        return [src, out.at[half, :, pl.ds(first, count)]]

    def f_here(b):
        src, dst = handed(arecv.at[:, pl.ds(b * B, B)], B, b * B, core)
        return pltpu.make_async_copy(src, dst, f_local.at[0])

    def f_mate(b):
        src, dst = handed(arecv.at[:, pl.ds(b * B, B)], B, b * B, core)
        return remote(src, dst, f_send.at[0], f_recv.at[0], peer)

    def spread(b):
        f_here(b).start()
        f_mate(b).start()

    for s in range(CAP):
        o_arrive(s).wait_recv()
    for way in range(2):
        for i in range(Z):
            shadow[way, i] = own4[way, ag_ref[i]]
    src, dst = handed(own4, 2 * CAP * Q, M, core)
    t_here = pltpu.make_async_copy(src, dst, t_local.at[0])
    t_mate = remote(src, dst, t_send.at[0], t_recv.at[0], peer)
    t_here.start()
    t_mate.start()

    stream(a_copy, arecv, lambda way, j: shadow[way, Z + j - lag_ref[2]], spread)

    for way in range(2):
        remote(ssend.at[way], arecv.at[way], a_send.at[way], a_recv.at[way, 0], z_to[way]).wait_send()
    src, dst = handed(arecv, M, 0, core)
    pltpu.make_async_copy(src, dst, f_local.at[0]).wait()
    remote(src, dst, f_send.at[0], f_recv.at[0], peer).wait_send()
    src, dst = handed(arecv, M, 0, mate)
    remote(src, dst, f_send.at[0], f_recv.at[0], peer).wait_recv()
    t_here.wait()
    t_mate.wait_send()
    src, dst = handed(own4, 2 * CAP * Q, M, mate)
    remote(src, dst, t_send.at[0], t_recv.at[0], peer).wait_recv()
    for buf, send, to in ((hb, x_send, x_to), (gb, y_send, y_to)):
        sent = buf.at[:, pl.ds(0, 3 * TOK)]
        remote(sent, sent, send.at[0], send.at[0], to[0]).wait_send()
    remote(pb.at[:, mate], eb, pe_send.at[0], pe_recv.at[0], peer).wait_send()
    for s in range(CAP):
        gx_copy(s).wait_send()
        o_copy(s).wait_send()


def run_main(owners, hidden, grad_out, left_stat, right_stat, left_root, right_root):
    dma = pltpu.SemaphoreType.DMA
    anywhere = pl.BlockSpec(memory_space=pl.ANY)
    scalars = pl.BlockSpec(memory_space=pltpu.SMEM)
    stream = pltpu.VMEM((2, M, ROWS, BLOCK), BF16)

    def table(size):
        return pltpu.SMEM((size,), jnp.int32)

    return pl.pallas_call(
        main_kernel,
        out_shape=(
            jax.ShapeDtypeStruct((2, 2, M + 2 * CAP * Q, ROWS, BLOCK), BF16),
            jax.ShapeDtypeStruct((2 * NB,), jnp.int32),
        ),
        in_specs=[scalars] + [anywhere] * 6,
        out_specs=(anywhere, scalars),
        scratch_shapes=[
            pltpu.VMEM((BR, 4 * TOK, BLOCK), BF16),
            pltpu.VMEM((BC, 4 * TOK, BLOCK), BF16),
            pltpu.VMEM((NB, 2, 2 * Q, ROWS, BLOCK), BF16),
            pltpu.VMEM((NB, 2 * Q, ROWS, BLOCK), BF16),
            pltpu.VMEM((2, NB * Q, ROWS, BLOCK), BF16),
            stream,
            stream,
            stream,
            pltpu.VMEM((2, Z + M, ROWS, BLOCK), BF16),
            pltpu.VMEM((CAP, 2, 2 * Q, ROWS, BLOCK), BF16),
            pltpu.VMEM((CAP, 2 * Q, ROWS, BLOCK), BF16),
            pltpu.VMEM((2, 2 * CAP * Q, ROWS, BLOCK), BF16),
            pltpu.VMEM((CAP, 2, 2, Q, ROWS, BLOCK), BF16),
            pltpu.VMEM((4, CAP, BLOCK, BLOCK), BF16),
            pltpu.VMEM((CAP, 4, BLOCK, BLOCK), BF16),
            pltpu.VMEM((CAP, BLOCK, BLOCK), F32),
            pltpu.VMEM((BR, BLOCK, BLOCK), F32),
            table(CHIPS), table(CHIPS), table(2 * M), table(4 * CAP), table(2 * CAP), table(Z), table(3),
            dma((11,)),
            dma((1,)), dma((BR, 4)), dma((1,)), dma((BC, 4)),
            dma((1,)), dma((NB,)),
            dma((2,)), dma((2, R)), dma((2,)), dma((2, R)),
            dma((CAP,)), dma((CAP,)), dma((CAP,)), dma((CAP,)),
            dma((1,)), dma((1,)), dma((1,)),
            dma((1,)), dma((1,)), dma((1,)),
        ],
        compiler_params=pltpu.CompilerParams(
            collective_id=0, has_side_effects=True, vmem_limit_bytes=62 * 1024 * 1024
        ),
        name="main",
    )(owners, hidden, grad_out, left_stat, right_stat, left_root, right_root)


def lay_out_kernel(pos, pieces, out, buf, in_sem, out_sem):
    def reads(k):
        return [
            pltpu.make_async_copy(
                pieces.at[half, way, pl.ds(pos[way * NB + k], Q)], buf.at[k, half, way], in_sem.at[k, half, way]
            )
            for half in range(2)
            for way in range(2)
        ]

    def write(k):
        r, c = k // BC, k % BC
        return pltpu.make_async_copy(
            buf.at[k].reshape(BLOCK, BLOCK),
            out.at[pl.ds(r * BLOCK, BLOCK), pl.ds(c * BLOCK, BLOCK)],
            out_sem.at[k],
        )

    for k in range(NB):
        for copy in reads(k):
            copy.start()
    for k in range(NB):
        for copy in reads(k):
            copy.wait()
        write(k).start()
    for k in range(NB):
        write(k).wait()


def run_lay_out(pos, pieces):
    dma = pltpu.SemaphoreType.DMA
    return pl.pallas_call(
        lay_out_kernel,
        out_shape=jax.ShapeDtypeStruct((BR * BLOCK, BC * BLOCK), BF16),
        in_specs=[pl.BlockSpec(memory_space=pltpu.SMEM), pl.BlockSpec(memory_space=pl.ANY)],
        out_specs=pl.BlockSpec(memory_space=pl.ANY),
        scratch_shapes=[
            pltpu.VMEM((NB, 2, 2, Q, ROWS, BLOCK), BF16),
            dma((NB, 2, 2)),
            dma((NB,)),
        ],
        compiler_params=pltpu.CompilerParams(vmem_limit_bytes=60 * 1024 * 1024),
        name="lay_out",
    )(pos, pieces)


def shards(hidden, grad_out, block_owner, left_stat, right_stat, left_root, right_root):
    pieces, pos = run_main(
        block_owner.reshape(NB), hidden, grad_out, left_stat, right_stat, left_root, right_root
    )
    return run_lay_out(pos, pieces)


def solution(mesh):
    in_specs = (
        P(("dp", "pre"), "mp"),
        P(("dp", "mp"), "pre"),
        P("mp", "pre", None, None),
        P("dp", "mp", "pre"),
        P("dp", "mp", "pre"),
        P("dp", "mp", "pre"),
        P("dp", "mp", "pre"),
    )
    return jax.shard_map(
        shards, mesh=mesh, in_specs=in_specs, out_specs=P("mp", "pre"), check_vma=False
    )
```
